32 devices in a mesh: outer: 4 (over x, core), dp: 4 (over z), mp: 2 (over y).
Axes of the slice: x: 2, y: 2, z: 4, core: 2. Of those that a mesh axis runs over, the one named last changes fastest.
Arguments:
- tokens: bfloat16 [4, 4096, 2048], P('outer', 'dp'), may hold values from -6 to 6
- cotangent: bfloat16 [4, 4096, 2048], P('outer', 'dp'), may hold values from -0.59765625 to 0.59765625
- gate_weight: bfloat16 [4, 2048, 6144], P('outer', 'dp', 'mp'), may hold values from -0.125 to 0.125
- up_weight: bfloat16 [4, 2048, 6144], P('outer', 'dp', 'mp'), may hold values from -0.125 to 0.125
- down_master: float32 [4, 6144, 2048], P('outer', 'mp', 'dp'), may hold values from -0.0375 to 0.0375
- first_moment: float32 [4, 6144, 2048], P('outer', 'mp', 'dp'), may hold values from -0.6 to 0.6
- second_moment: float32 [4, 6144, 2048], P('outer', 'mp', 'dp'), may hold values from 1 to 10
- anchor: float32 [6144, 2048], P('mp', 'dp'), may hold values from -0.0375 to 0.0375
- outer_momentum: float32 [6144, 2048], P('mp', 'dp'), may hold values from -0.00018 to 0.00018
Outputs:
- new_params: float32 [6144, 2048], P('mp', 'dp')
- first_out: float32 [4, 6144, 2048], P('outer', 'mp', 'dp')
- second_out: float32 [4, 6144, 2048], P('outer', 'mp', 'dp')
- momentum_out: float32 [6144, 2048], P('mp', 'dp')
- input_grad: bfloat16 [4, 4096, 2048], P('outer', ('dp', 'mp'))
The draws below stay inside these ranges and needn't reach their ends.
All inputs are finite; a program needn't handle non-finite values.
Results may differ from the reference program's by a relative error of at most 0.023.
Values may be sent and summed in bfloat16 or wider, within the bound.
A program may use at most 256 MiB of HBM per device.

```python
import math
import jax
import jax.numpy as jnp

D = 2048
FF = 6144
TOKENS = 4096
REPLICAS = 4
N_OUTER = 4
N_MP = 2


def base_field(key):
    values = jax.random.normal(jax.random.fold_in(key, 17), (FF, D), jnp.float32)
    return 0.0125 * jnp.clip(values, -3.0, 3.0)


def draw_anchor(key, part):
    return base_field(key)


def draw_down_master(key, part):
    wander = 1e-05 * jax.random.normal(jax.random.fold_in(key, 29), (REPLICAS, FF, D), jnp.float32)
    return jnp.clip(base_field(key)[None] + wander, -0.0375, 0.0375)


def level_of(rng, shape, cuts, smallest, high):
    def one(axis_at, parts):
        draws = jax.random.uniform(jax.random.fold_in(jax.random.fold_in(rng, 6), axis_at), (parts,), jnp.float32, smallest / len(cuts), high / len(cuts))
        return jnp.repeat(jnp.exp(draws), shape[axis_at] // parts).reshape((-1,) + (1,) * (len(shape) - axis_at - 1))

    level = one(*cuts[0])
    for cut in cuts[1:]:
        level = level * one(*cut)
    return level


def centred(stream_key, extent, width, limit, pieces=(), dtype=jnp.bfloat16):
    entries = width * jax.random.normal(stream_key, extent, jnp.float32)
    if pieces:
        entries = entries * level_of(stream_key, extent, pieces, -0.22, 0.18)
    return jnp.clip(entries, -limit, limit).astype(dtype)


def setup_inputs(seed: int = 0) -> dict:
    keys = jax.random.split(jax.random.key(seed), 10)
    return {
        "tokens": centred(keys[0], (REPLICAS, TOKENS, D), 1.0, 6.0, ((0, 4), (1, 4))),
        "cotangent": centred(keys[1], (REPLICAS, TOKENS, D), 0.1, 0.59765625, ((0, 4), (1, 4))),
        "gate_weight": centred(keys[2], (REPLICAS, D, FF), D ** -0.5, 0.125, ((0, 4), (1, 4), (2, 2))),
        "up_weight": centred(keys[3], (REPLICAS, D, FF), D ** -0.5, 0.125, ((0, 4), (1, 4), (2, 2))),
        "down_master": draw_down_master(jax.random.fold_in(keys[9], 71), 0),
        "first_moment": centred(keys[5], (REPLICAS, FF, D), 0.1, 0.6, ((0, 4), (1, 2), (2, 4)), jnp.float32),
        "second_moment": jnp.clip(jnp.exp(math.log(10.0) - 2.3025851 * jax.random.uniform(keys[6], (REPLICAS, FF, D), jnp.float32) ** level_of(keys[6], (REPLICAS, FF, D), ((0, 4), (1, 2), (2, 4)), -0.2, 0.2)), 1.0, 10.0),
        "anchor": draw_anchor(jax.random.fold_in(keys[9], 71), 0),
        "outer_momentum": centred(keys[8], (FF, D), 0.00003, 0.00018, ((0, 2), (1, 4)), jnp.float32),
    }


bias_one = 1.0 - (0.9 ** 50) ** 2
bias_two = 1.0 - (0.999 ** 50) ** 2

def replica_drift(inputs, upstream, gate_w, up_w, master, moment_one, moment_two, anchor):
    gate_pre = jnp.dot(inputs, gate_w, preferred_element_type=jnp.float32)
    up_pre = jnp.dot(inputs, up_w, preferred_element_type=jnp.float32)
    gate_sigmoid = jax.nn.sigmoid(gate_pre)
    active = gate_pre * gate_sigmoid
    hidden = (active * up_pre).astype(jnp.bfloat16)
    down_half = master.astype(jnp.bfloat16)
    grad_hidden = jnp.dot(upstream, down_half.T, preferred_element_type=jnp.float32)
    grad_up = (grad_hidden * active).astype(jnp.bfloat16)
    grad_gate = (grad_hidden * up_pre * gate_sigmoid * (1.0 + gate_pre * (1.0 - gate_sigmoid))).astype(jnp.bfloat16)
    block_width = FF // N_MP
    summed = jnp.zeros((inputs.shape[0], inputs.shape[1]), jnp.float32)
    for block_idx in range(N_MP):
        lower = block_idx * block_width
        upper = lower + block_width
        partial_term = jnp.dot(grad_gate[:, lower:upper], gate_w[:, lower:upper].T, preferred_element_type=jnp.float32)
        partial_term = partial_term + jnp.dot(grad_up[:, lower:upper], up_w[:, lower:upper].T, preferred_element_type=jnp.float32)
        summed = summed + partial_term.astype(jnp.bfloat16).astype(jnp.float32)
    input_grad = summed.astype(jnp.bfloat16)
    grad_down = jnp.dot(hidden.T, upstream, preferred_element_type=jnp.float32)
    first_new = 0.9 * moment_one + 0.1 * grad_down
    second_new = 0.999 * moment_two + 0.001 * grad_down * grad_down
    adam_step = first_new / bias_one / (jnp.sqrt(second_new / bias_two) + 1e-08) + 0.1 * master
    inner_params = master - 0.001 * adam_step
    return (anchor - inner_params, first_new, second_new, input_grad)

def reference(tokens, cotangent, gate_weight, up_weight, down_master, first_moment, second_moment, anchor, outer_momentum):
    drift_total = jnp.zeros(anchor.shape, jnp.float32)
    firsts = []
    seconds = []
    grads = []
    for replica in range(N_OUTER):
        drift_local, first_new, second_new, input_grad = replica_drift(tokens[replica], cotangent[replica], gate_weight[replica], up_weight[replica], down_master[replica], first_moment[replica], second_moment[replica], anchor)
        drift_total = drift_total + drift_local
        firsts.append(first_new)
        seconds.append(second_new)
        grads.append(input_grad)
    mean_drift = drift_total / N_OUTER
    momentum_out = 0.9 * outer_momentum + mean_drift
    new_params = anchor - 0.7 * (mean_drift + 0.9 * momentum_out)
    return (new_params, jnp.stack(firsts), jnp.stack(seconds), momentum_out, jnp.stack(grads))
```

```python
import jax
import jax.numpy as jnp
from jax import lax
from jax.sharding import PartitionSpec as P

bias_one = 1.0 - (0.9**50) ** 2
bias_two = 1.0 - (0.999**50) ** 2

chunks = 2
depth = 2


def swap(value, axis, bit):
    pairs = [(i, i ^ bit) for i in range(4)]
    return lax.ppermute(value, axis, pairs)


def cut(value, start, size, axis):
    return lax.dynamic_slice_in_dim(value, start, size, axis)


def reorder(value, me):
    width = value.shape[1] // 4
    return jnp.concatenate(
        [cut(value, (me ^ k) * width, width, 1) for k in range(4)], axis=1
    )


def dot(a, b, ca, cb):
    return lax.dot_general(a, b, (((ca,), (cb,)), ((), ())), preferred_element_type=jnp.float32)


def shards(
    tokens,
    cotangent,
    gate_weight,
    up_weight,
    down_master,
    first_moment,
    second_moment,
    anchor,
    outer_momentum,
):
    me = lax.axis_index("dp")
    parity = me % 2
    mp_size = lax.axis_size("mp")
    mine_mp = lax.axis_index("mp")
    half = gate_weight.shape[2] // 2
    part = half // chunks
    rows = tokens.shape[1]
    master = down_master[0]
    down_half = master.astype(jnp.bfloat16)

    queues = {"middle": [], "end": []}

    def send(value, bit, queue, after=()):
        done = queues[queue]
        before = tuple(done[-depth : len(done) - depth + 1]) if len(done) >= depth else ()
        before = before + tuple(after)
        if before:
            value = lax.optimization_barrier((value,) + before)[0]
        result = swap(value, "dp", bit)
        done.append(result)
        return result

    def share(block):
        piece = cut(block, mine_mp * (rows // mp_size), rows // mp_size, 0)
        other = lax.all_gather(send(piece, 1, "end"), "mp", axis=0, tiled=True)
        return reorder(jnp.concatenate([block, other], axis=0), me)

    def gather(shard, axis, c, after=()):
        keep = cut(shard, (2 * c + parity) * part, part, axis)
        away = cut(shard, (2 * c + 1 - parity) * part, part, axis)
        far = [send(keep, 2, "middle"), send(away, 3, "middle", after)]
        pieces = [keep, send(away, 1, "end")] + far
        return jnp.concatenate(pieces, axis=1 - axis)

    inputs = share(tokens[0])
    upstream = share(cotangent[0])
    downs = [gather(down_half, 0, c) for c in range(chunks)]
    grad_hiddens = [dot(upstream, down, 1, 1) for down in downs]

    def term_of(grad_hidden, active, slope, gate_full, up_full):
        grad_up = (grad_hidden * active).astype(jnp.bfloat16)
        grad_gate = (grad_hidden * slope).astype(jnp.bfloat16)
        return dot(grad_gate, gate_full, 1, 1) + dot(grad_up, up_full, 1, 1)

    grads = []
    width = tokens.shape[2] // 4
    even = parity == 0
    total = None
    arrived = None
    full_grad = None
    for c in range(chunks):
        gate_full = gather(gate_weight[0], 1, c, grad_hiddens if c == 1 else ())
        up_full = gather(up_weight[0], 1, c, () if c == 0 else (full_grad,))
        if c > 0:
            up_full, total = lax.optimization_barrier((up_full, total))
        gate_pre = dot(inputs, gate_full, 1, 0)
        up_pre = dot(inputs, up_full, 1, 0)
        gate_sigmoid = jax.nn.sigmoid(gate_pre)
        active = gate_pre * gate_sigmoid
        slope = up_pre * gate_sigmoid * (1.0 + gate_pre * (1.0 - gate_sigmoid))
        hidden = (active * up_pre).astype(jnp.bfloat16)
        full_grad = dot(hidden, upstream, 0, 0).astype(jnp.bfloat16)
        if c == 0:
            total = term_of(grad_hiddens[c], active, slope, gate_full, up_full)
            grads.append(full_grad)
        else:
            grads.append(full_grad)
            front = (grad_hiddens[c], active, slope, gate_full, up_full)

    for c in range(chunks):
        full_grad = grads[c]
        arrived = send(full_grad[:, 2 * width :], 2, "middle")
        if c == 0:
            grad_hidden = lax.optimization_barrier((front[0], arrived, grads[1]))[0]
            total = total + term_of(grad_hidden, *front[1:])
        summed = full_grad[:, : 2 * width].astype(jnp.float32) + arrived.astype(jnp.float32)
        came = swap(summed[:, width:].astype(jnp.bfloat16), "dp", 1).astype(jnp.float32)
        kept = summed[:, :width]
        grads[c] = jnp.concatenate(
            [jnp.where(even, kept, came), jnp.where(even, came, kept)], axis=0
        )

    partial = reorder(total.astype(jnp.bfloat16), me)
    split = partial.reshape(2, mp_size, rows // mp_size, partial.shape[1])
    own, other = split[0], split[1]
    other_sum = lax.psum_scatter(other, "mp", scatter_dimension=0, tiled=True)[0]
    other_back = swap(other_sum, "dp", 1)
    own_sum = lax.psum_scatter(own, "mp", scatter_dimension=0, tiled=True)[0]
    input_grad = (own_sum.astype(jnp.float32) + other_back.astype(jnp.float32)).astype(
        jnp.bfloat16
    )

    def adam(grad_down, low, high):
        first_new = 0.9 * first_moment[0, low:high] + 0.1 * grad_down
        second_new = 0.999 * second_moment[0, low:high] + 0.001 * grad_down * grad_down
        return first_new, second_new

    core = lax.axis_index("outer") % 2
    first_core = core == 0
    means = []
    for c in range(chunks):
        low, high = 2 * c * part, 2 * (c + 1) * part
        first_new, second_new = adam(grads[c], low, high)
        adam_step = (
            first_new / bias_one / (jnp.sqrt(second_new / bias_two) + 1e-08)
            + 0.1 * master[low:high]
        )
        inner_params = master[low:high] - 0.001 * adam_step
        drift = (anchor[low:high] - inner_params).astype(jnp.bfloat16)
        near = cut(drift, core * part, part, 0)
        pair = near.astype(jnp.float32) + swap(
            cut(drift, (1 - core) * part, part, 0), "outer", 1
        ).astype(jnp.float32)
        pair = pair.astype(jnp.bfloat16)
        quad = pair.astype(jnp.float32) + swap(pair, "outer", 2).astype(jnp.float32)
        quad = quad.astype(jnp.bfloat16)
        back = swap(quad, "outer", 1)
        means += [jnp.where(first_core, quad, back), jnp.where(first_core, back, quad)]

    first_new, second_new = adam(jnp.concatenate(grads, axis=0), 0, master.shape[0])
    mean_drift = jnp.concatenate(means, axis=0).astype(jnp.float32) / 4.0
    momentum_out = 0.9 * outer_momentum + mean_drift
    new_params = anchor - 0.7 * (mean_drift + 0.9 * momentum_out)
    return (new_params, first_new[None], second_new[None], momentum_out, input_grad[None])


def solution(mesh):
    return jax.shard_map(
        shards,
        mesh=mesh,
        in_specs=(
            P("outer", "dp", None),
            P("outer", "dp", None),
            P("outer", "dp", "mp"),
            P("outer", "dp", "mp"),
            P("outer", "mp", "dp"),
            P("outer", "mp", "dp"),
            P("outer", "mp", "dp"),
            P("mp", "dp"),
            P("mp", "dp"),
        ),
        out_specs=(
            P("mp", "dp"),
            P("outer", "mp", "dp"),
            P("outer", "mp", "dp"),
            P("mp", "dp"),
            P("outer", ("dp", "mp"), None),
        ),
        check_vma=False,
    )
```
